32 devices in a mesh: virt: 8 (over y, x, core), opair: 4 (over z).
Axes of the slice: x: 2, y: 2, z: 4, core: 2. Of those that a mesh axis runs over, the one named last changes fastest.
Arguments:
- amplitudes: bfloat16 [64, 6144], P('virt', 'opair'), may hold values from -6 to 6
- integrals: bfloat16 [6144, 1024, 128], P('opair', 'virt'), may hold values from -0.078125 to 0.078125
- driver: bfloat16 [64, 1024, 128], P('opair', 'virt'), may hold values from -6 to 6
- eps_occ: float32 [200], replicated, may hold values from -2 to -0.5
- eps_vir: float32 [1024], replicated, may hold values from 0.2 to 2
- pair_occ: int32 [64, 2], P('opair'), may hold values from 0 to 199
- offsets: int32 [1024], P('virt'), may hold values from 0 to 896, as said below
- sizes: int32 [1024], P('virt'), may hold values from 64 to 128, as said below
Outputs:
- update: bfloat16 [64, 1024, 128], P('opair', 'virt')
The draws below stay inside these ranges and needn't reach their ends.
Inputs may be any that keep to these rules, and one draw needn't show every extreme that they name: There are 8 irrep blocks, block k starting at k * 128; a's block starts at offsets[a], and every block is paired with some a. sizes[a] is the length of a's block; 128 is reached by some block in every draw.
All inputs are finite; a program needn't handle non-finite values.
Results may differ from the reference program's by a relative error of at most 0.001.
Values may be sent and summed in bfloat16 or wider, within the bound.
A program may use at most 128 MiB of HBM per device.

```python
import jax
import jax.numpy as jnp

NVIR = 1024
NOCC = 200
BMAX = 128
NPAIR = 64
NSLAB = 6144


def irrep_tables(key):
    base = jax.random.fold_in(key, 4242)
    count_key = jax.random.fold_in(base, 1)
    wide_key = jax.random.fold_in(base, 2)
    label_key = jax.random.fold_in(base, 3)
    counts = jax.random.randint(count_key, (8,), BMAX // 2, BMAX + 1, dtype=jnp.int32)
    widest = jax.random.randint(wide_key, (), 0, 8, dtype=jnp.int32)
    counts = jnp.where(jnp.arange(8, dtype=jnp.int32) == widest, jnp.int32(BMAX), counts)
    starts = (jnp.arange(8, dtype=jnp.int32) * BMAX).astype(jnp.int32)
    labels = jax.random.randint(label_key, (NVIR,), 0, 8, dtype=jnp.int32)
    position = jnp.arange(NVIR, dtype=jnp.int32)
    labels = jnp.where(position < 8, position, labels).astype(jnp.int32)
    return (jnp.take(starts, labels).astype(jnp.int32), jnp.take(counts, labels).astype(jnp.int32))


def draw_offsets(key, part):
    return irrep_tables(key)[0]


def draw_sizes(key, part):
    return irrep_tables(key)[1]


def with_ends(array, stream_key, least, top_value):
    extent = array.shape
    spot = [jax.random.randint(jax.random.fold_in(stream_key, axis), (), 0, extent[axis]) for axis in range(len(extent))]
    array = array.at[tuple(spot)].set(least)
    longest = extent.index(max(extent))
    spot[longest] = (spot[longest] + 1) % extent[longest]
    return array.at[tuple(spot)].set(top_value)


def block_levels(key, extent, split, smallest, high):
    def one(dim, blocks):
        draws = jax.random.uniform(jax.random.fold_in(jax.random.fold_in(key, 6), dim), (blocks,), jnp.float32, smallest / len(split), high / len(split))
        return jnp.repeat(jnp.exp(draws), extent[dim] // blocks).reshape((-1,) + (1,) * (len(extent) - dim - 1))

    gain = one(*split[0])
    for cut in split[1:]:
        gain = gain * one(*cut)
    return gain


def normal_values(key, shape, spread, limit, pieces=(), held_as=jnp.bfloat16):
    entries = spread * jax.random.normal(key, shape, jnp.float32)
    if pieces:
        entries = entries * block_levels(key, shape, pieces, -0.22, 0.18)
    return jnp.clip(entries, -limit, limit).astype(held_as)


def setup_inputs(seed: int = 0) -> dict:
    splits = jax.random.split(jax.random.key(seed), 9)
    return {
        "amplitudes": normal_values(splits[0], (NPAIR, NSLAB), 1.0, 6.0, ((0, 8), (1, 4))),
        "integrals": normal_values(splits[1], (NSLAB, NVIR, BMAX), NSLAB ** -0.5, 0.078125, ((0, 4), (1, 8))),
        "driver": normal_values(splits[2], (NPAIR, NVIR, BMAX), 1.0, 6.0, ((0, 4), (1, 8))),
        "eps_occ": jnp.clip(jax.random.uniform(splits[3], (NOCC,), jnp.float32, -2.0, -0.5), -2.0, -0.5),
        "eps_vir": jnp.clip(jax.random.uniform(splits[4], (NVIR,), jnp.float32, 0.2, 2.0), 0.2, 2.0),
        "pair_occ": with_ends(jax.random.randint(splits[5], (NPAIR, 2), 0, NOCC), jax.random.fold_in(splits[5], 1), 0, NOCC - 1).astype(jnp.int32),
        "offsets": draw_offsets(jax.random.fold_in(splits[8], 71), 0),
        "sizes": draw_sizes(jax.random.fold_in(splits[8], 71), 0),
    }


def reference(amplitudes, integrals, driver, eps_occ, eps_vir, pair_occ, offsets, sizes):
    flat = integrals.reshape(NSLAB, NVIR * BMAX)
    ladder = jnp.dot(amplitudes, flat, preferred_element_type=jnp.float32).reshape(NPAIR, NVIR, BMAX)
    pair_energy = jnp.take(eps_occ, pair_occ[:, 0]) + jnp.take(eps_occ, pair_occ[:, 1])
    column = jnp.arange(BMAX, dtype=jnp.int32)
    b_index = (offsets[:, None] + jnp.minimum(column[None, :], sizes[:, None] - 1)).astype(jnp.int32)
    e_pair = jnp.take(eps_vir, b_index)
    denominator = pair_energy[:, None, None] - eps_vir[None, :, None] - e_pair[None, :, :]
    value = (ladder + driver.astype(jnp.float32)) / denominator
    inside = column[None, None, :] < sizes[None, :, None]
    return jnp.where(inside, value, jnp.zeros_like(value)).astype(jnp.bfloat16)
```

```python
import functools

import jax
import jax.numpy as jnp
from jax import lax
from jax.experimental import pallas as pl
from jax.experimental.pallas import tpu as pltpu
from jax.sharding import PartitionSpec as P

MESH = pl.DeviceIdType.MESH
LANES = 128
LEVELS = 32000.0


def encode(x, out_ref, width):
    top = jnp.maximum(jnp.max(jnp.abs(x), axis=1, keepdims=True), 1e-30)
    code = jnp.broadcast_to(jnp.ceil(jnp.log2(top) * 64.0), (x.shape[0], LANES))
    gain = (jnp.exp2(code * (-1.0 / 64.0)) * LEVELS)[:, :1]
    out_ref[:, :width] = jnp.round(x * gain).astype(jnp.int32).astype(jnp.int16)
    out_ref[:, width:] = code.astype(jnp.int32).astype(jnp.int16)


def decode(in_ref, width):
    code = in_ref[:, width:].astype(jnp.int32).astype(jnp.float32)
    gain = (jnp.exp2(code * (1.0 / 64.0)) * (1.0 / LEVELS))[:, :1]
    return in_ref[:, :width].astype(jnp.int32).astype(jnp.float32) * gain


def kernel(
    n, nv, step_rows, slots,
    amp_ref, int_ref, driver_ref, pe_ref, ef_ref, ep_ref, in_ref, out_ref,
    panel32, panel, ibuf, acc, sbuf, rbuf,
    isem, asend, arecv, ssem, rsem,
):
    z = lax.axis_index("opair")
    v = lax.axis_index("virt")
    chunks, pairs, width = acc.shape
    rows = pairs // n
    slab, ca = ibuf.shape[1], ibuf.shape[2]
    last = n - 1

    def load(c):
        slot = lax.rem(c, slots)
        return pltpu.make_async_copy(
            int_ref.at[:, pl.ds(pl.multiple_of(c * ca, ca), ca), :], ibuf.at[slot], isem.at[slot]
        )

    for c in range(min(slots, chunks)):
        load(c).start()

    barrier = pltpu.get_barrier_semaphore()

    def greet(d, carry):
        peer = lax.rem(v + d, nv)
        pl.semaphore_signal(barrier, inc=1, device_id={"virt": peer}, device_id_type=MESH)
        return carry

    lax.fori_loop(1, nv, greet, 0)

    @pl.when(z > 0)
    def _():
        pl.semaphore_signal(barrier, inc=1, device_id={"opair": z - 1}, device_id_type=MESH)

    @pl.when(z < last)
    def _():
        pl.semaphore_signal(barrier, inc=1, device_id={"opair": z + 1}, device_id_type=MESH)

    panel32[v] = amp_ref[...].astype(jnp.float32)
    beside = jnp.where(z > 0, 1, 0) + jnp.where(z < last, 1, 0)
    pl.semaphore_wait(barrier, nv - 1 + beside)

    def share(d, slot):
        peer = lax.rem(v + d, nv)
        return pltpu.make_async_remote_copy(
            src_ref=panel32.at[slot],
            dst_ref=panel32.at[slot],
            send_sem=asend.at[d],
            recv_sem=arecv.at[d],
            device_id={"virt": peer},
            device_id_type=MESH,
        )

    def start_share(d, carry):
        share(d, v).start()
        return carry

    def wait_share(d, carry):
        share(d, lax.rem(v - d + nv, nv)).wait_recv()
        return carry

    def done_share(d, carry):
        share(d, v).wait_send()
        return carry

    lax.fori_loop(1, nv, start_share, 0)
    lax.fori_loop(1, nv, wait_share, 0)
    panel[...] = panel32[...].reshape(pairs, slab).astype(jnp.bfloat16)

    def message(side, c, t):
        peer = lax.rem(z + 1, n) if side == 0 else lax.rem(z + last, n)
        return pltpu.make_async_remote_copy(
            src_ref=sbuf.at[side, c, t - 1],
            dst_ref=rbuf.at[side, c, t - 1],
            send_sem=ssem.at[side, c, t - 1],
            recv_sem=rsem.at[side, c, t - 1],
            device_id={"opair": peer},
            device_id_type=MESH,
        )

    def part(c, owner):
        return acc[c, pl.ds(pl.multiple_of(owner * rows, rows), rows), :]

    def place(side):
        return z if side == 0 else last - z

    def owner_of(side, t):
        o = place(side) + n - t
        return o if side == 0 else last - o

    def compute(c):
        load(c).wait()
        slot = lax.rem(c, slots)
        acc[c] = jnp.zeros((pairs, width), jnp.float32)

        def step(k, carry):
            at = pl.multiple_of(k * step_rows, step_rows)
            block = ibuf[slot, pl.ds(at, step_rows)].reshape(step_rows, width)
            acc[c] += jnp.dot(
                panel[:, pl.ds(at, step_rows)], block, preferred_element_type=jnp.float32
            )
            return carry

        lax.fori_loop(0, slab // step_rows, step, 0)

        @pl.when(c + slots < chunks)
        def _():
            load(c + slots).start()

        for side in (0, 1):
            @pl.when(place(side) == 0)
            def _():
                for t in range(1, n):
                    encode(part(c, owner_of(side, t)), sbuf.at[side, c, t - 1], width)
                    message(side, c, t).start()

    def forward(c, t):
        for side in (0, 1):
            @pl.when((place(side) > 0) & (place(side) < t))
            def _():
                message(side, c, t - 1).wait_recv()
                total = part(c, owner_of(side, t)) + decode(rbuf.at[side, c, t - 2], width)
                encode(total, sbuf.at[side, c, t - 1], width)
                message(side, c, t).start()

    def finish(c):
        for side in (0, 1):
            @pl.when(place(side) > 0)
            def _():
                message(side, c, n - 1).wait_recv()
                at = pl.ds(pl.multiple_of(z * rows, rows), rows)
                acc[c, at, :] += decode(rbuf.at[side, c, n - 2], width)
        denominator = pe_ref[...] - ef_ref[c] - ep_ref[c]
        value = (part(c, z) + driver_ref[c].astype(jnp.float32)) / denominator
        out_ref[c] = jnp.where(in_ref[c] > 0, value, 0.0).astype(jnp.bfloat16)

    end_lag = n

    def turn(i, carry):
        @pl.when(i < chunks)
        def _():
            compute(i)

        for t in range(2, n):
            c = i - (t - 1)

            @pl.when((c >= 0) & (c < chunks))
            def _():
                forward(c, t)

        c = i - end_lag

        @pl.when(c >= 0)
        def _():
            finish(c)

        return carry

    lax.fori_loop(0, chunks + end_lag, turn, 0)
    lax.fori_loop(1, nv, done_share, 0)

    def done(c, carry):
        for side in (0, 1):
            for t in range(1, n):
                @pl.when((place(side) < t) & (place(side) < last))
                def _():
                    message(side, c, t).wait_send()
        return carry

    lax.fori_loop(0, chunks, done, 0)


def local(n, nv, amplitudes, integrals, driver, eps_occ, eps_vir, pair_occ, offsets, sizes):
    slab, a_count, bwidth = integrals.shape
    rows = driver.shape[0]
    pairs = rows * n
    ca = 16 if a_count % 16 == 0 else a_count
    chunks = a_count // ca
    width = ca * bwidth
    step_rows = 256 if slab % 256 == 0 else slab
    slots = min(4, chunks)

    hit = pair_occ[:, :, None] == jnp.arange(eps_occ.shape[0], dtype=jnp.int32)
    each = jnp.sum(jnp.where(hit, eps_occ, 0.0), axis=2)
    pair_energy = each[:, 0:1] + each[:, 1:2]
    e_pair = jnp.zeros((a_count, bwidth), jnp.float32)
    for k in range(eps_vir.shape[0] // bwidth):
        e_pair = jnp.where(
            (offsets == k * bwidth)[:, None], eps_vir[None, k * bwidth:(k + 1) * bwidth], e_pair
        )
    first = lax.axis_index("virt") * a_count
    e_first = lax.dynamic_slice_in_dim(eps_vir, first, a_count, 0)
    column = jnp.arange(bwidth, dtype=jnp.int32)
    inside = (column[None, :] < sizes[:, None]).astype(jnp.float32)
    e_first = jnp.broadcast_to(e_first[:, None], (a_count, bwidth))

    def flat(x):
        return x.reshape(chunks, 1, width)

    driver = driver.reshape(rows, chunks, width).transpose(1, 0, 2)
    vmem = pl.BlockSpec(memory_space=pltpu.VMEM)
    out = pl.pallas_call(
        functools.partial(kernel, n, nv, step_rows, slots),
        out_shape=jax.ShapeDtypeStruct((chunks, rows, width), jnp.bfloat16),
        in_specs=[vmem, pl.BlockSpec(memory_space=pl.ANY)] + [vmem] * 5,
        out_specs=vmem,
        scratch_shapes=[
            pltpu.VMEM((nv, pairs // nv, slab), jnp.float32),
            pltpu.VMEM((pairs, slab), jnp.bfloat16),
            pltpu.VMEM((slots, slab, ca, bwidth), jnp.bfloat16),
            pltpu.VMEM((chunks, pairs, width), jnp.float32),
            pltpu.VMEM((2, chunks, n - 1, rows, width + LANES), jnp.int16),
            pltpu.VMEM((2, chunks, n - 1, rows, width + LANES), jnp.int16),
            pltpu.SemaphoreType.DMA((slots,)),
            pltpu.SemaphoreType.DMA((nv,)),
            pltpu.SemaphoreType.DMA((nv,)),
            pltpu.SemaphoreType.DMA((2, chunks, n - 1)),
            pltpu.SemaphoreType.DMA((2, chunks, n - 1)),
        ],
        compiler_params=pltpu.CompilerParams(
            collective_id=0, has_side_effects=True, vmem_limit_bytes=56 * 1024 * 1024
        ),
        cost_estimate=pl.CostEstimate(
            flops=2 * pairs * slab * a_count * bwidth,
            bytes_accessed=2 * slab * a_count * bwidth,
            transcendentals=0,
        ),
    )(amplitudes, integrals, driver, pair_energy, flat(e_first), flat(e_pair), flat(inside))
    return out.transpose(1, 0, 2).reshape(rows, a_count, bwidth)


def solution(mesh):
    placed = (
        P("virt", "opair"),
        P("opair", "virt", None),
        P("opair", "virt", None),
        P(),
        P(),
        P("opair", None),
        P("virt"),
        P("virt"),
    )
    return jax.shard_map(
        functools.partial(local, mesh.shape["opair"], mesh.shape["virt"]),
        mesh=mesh, in_specs=placed, out_specs=P("opair", "virt", None), check_vma=False,
    )
```

```python
import functools

import jax
import jax.numpy as jnp
from jax import lax
from jax.experimental import pallas as pl
from jax.experimental.pallas import tpu as pltpu
from jax.sharding import PartitionSpec as P

MESH = pl.DeviceIdType.MESH
LANES = 128
LEVELS = 32000.0
OUTSIDE = 1e30


def encode(x, out_ref, width):
    top = jnp.maximum(jnp.max(jnp.abs(x), axis=1, keepdims=True), 1e-30)
    code = jnp.broadcast_to(jnp.ceil(jnp.log2(top) * 64.0), (x.shape[0], LANES))
    gain = (jnp.exp2(code * (-1.0 / 64.0)) * LEVELS)[:, :1]
    out_ref[:, :width] = jnp.round(x * gain).astype(jnp.int32).astype(jnp.int16)
    out_ref[:, width:] = code.astype(jnp.int32).astype(jnp.int16)


def decode(in_ref, width):
    code = in_ref[:, width:].astype(jnp.int32).astype(jnp.float32)
    gain = (jnp.exp2(code * (1.0 / 64.0)) * (1.0 / LEVELS))[:, :1]
    return in_ref[:, :width].astype(jnp.int32).astype(jnp.float32) * gain


def kernel(
    n, nv, step_rows, slots,
    amp_ref, int_ref, driver_ref, occ_ref, vir_ref, own_ref, pair_ref, off_ref, size_ref, out_ref,
    panel32, panel, ibuf, acc, sbuf, rbuf, pe_ref, base_ref,
    isem, asend, arecv, ssem, rsem,
):
    z = lax.axis_index("opair")
    v = lax.axis_index("virt")
    chunks, pairs, width = acc.shape
    rows = pairs // n
    slab, ca = ibuf.shape[1], ibuf.shape[2]
    last = n - 1

    bwidth = ibuf.shape[3]
    blocks = slab // step_rows

    def load(c, k):
        slot = lax.rem(c, slots)
        at = pl.ds(pl.multiple_of(k * step_rows, step_rows), step_rows)
        return pltpu.make_async_copy(
            int_ref.at[at, pl.ds(pl.multiple_of(c * ca, ca), ca), :], ibuf.at[slot, at], isem.at[slot, k]
        )

    for c in range(slots):
        for k in range(blocks):
            load(c, k).start()

    barrier = pltpu.get_barrier_semaphore()

    def greet(d, carry):
        peer = lax.rem(v + d, nv)
        pl.semaphore_signal(barrier, inc=1, device_id={"virt": peer}, device_id_type=MESH)
        return carry

    lax.fori_loop(1, nv, greet, 0)

    @pl.when(z > 0)
    def _():
        pl.semaphore_signal(barrier, inc=1, device_id={"opair": z - 1}, device_id_type=MESH)

    @pl.when(z < last)
    def _():
        pl.semaphore_signal(barrier, inc=1, device_id={"opair": z + 1}, device_id_type=MESH)

    panel32[v] = amp_ref[...].astype(jnp.float32)

    a_count = base_ref.shape[0]
    occupied = lax.broadcasted_iota(jnp.int32, (rows, occ_ref.shape[1]), 1)
    energy = jnp.zeros((rows, 1), jnp.float32)
    for j in (0, 1):
        hit = pair_ref[:, j:j + 1] == occupied
        energy += jnp.sum(jnp.where(hit, occ_ref[...], 0.0), axis=1, keepdims=True)
    pe_ref[...] = jnp.broadcast_to(energy, (rows, LANES))

    across = lax.broadcasted_iota(jnp.int32, (a_count, a_count), 1)
    same = lax.broadcasted_iota(jnp.int32, (a_count, a_count), 0) == across

    def column(x):
        return jnp.sum(jnp.where(same, x, 0.0), axis=1, keepdims=True)

    e_first = column(own_ref[pl.ds(v, 1), :])
    start = column(off_ref[...].astype(jnp.float32))
    size = column(size_ref[...].astype(jnp.float32))
    e_pair = jnp.zeros((a_count, bwidth), jnp.float32)
    for k in range(vir_ref.shape[0]):
        e_pair = jnp.where(start == float(k * bwidth), vir_ref[k:k + 1, :], e_pair)
    t_index = lax.broadcasted_iota(jnp.int32, (a_count, bwidth), 1).astype(jnp.float32)
    base_ref[...] = jnp.where(t_index < size, e_first + e_pair, OUTSIDE)
    beside = jnp.where(z > 0, 1, 0) + jnp.where(z < last, 1, 0)
    pl.semaphore_wait(barrier, nv - 1 + beside)

    def share(d, slot):
        peer = lax.rem(v + d, nv)
        return pltpu.make_async_remote_copy(
            src_ref=panel32.at[slot],
            dst_ref=panel32.at[slot],
            send_sem=asend.at[d],
            recv_sem=arecv.at[d],
            device_id={"virt": peer},
            device_id_type=MESH,
        )

    def start_share(d, carry):
        share(d, v).start()
        return carry

    def wait_share(d, carry):
        share(d, lax.rem(v - d + nv, nv)).wait_recv()
        return carry

    def done_share(d, carry):
        share(d, v).wait_send()
        return carry

    lax.fori_loop(1, nv, start_share, 0)
    lax.fori_loop(1, nv, wait_share, 0)
    panel[...] = panel32[...].reshape(pairs, slab).astype(jnp.bfloat16)

    def message(side, c, t):
        peer = lax.rem(z + 1, n) if side == 0 else lax.rem(z + last, n)
        return pltpu.make_async_remote_copy(
            src_ref=sbuf.at[side, c, t - 1],
            dst_ref=rbuf.at[side, c, t - 1],
            send_sem=ssem.at[side, c, t - 1],
            recv_sem=rsem.at[side, c, t - 1],
            device_id={"opair": peer},
            device_id_type=MESH,
        )

    def part(c, owner):
        return acc[c, pl.ds(pl.multiple_of(owner * rows, rows), rows), :]

    def place(side):
        return z if side == 0 else last - z

    def owner_of(side, t):
        o = place(side) + n - t
        return o if side == 0 else last - o

    def compute(c):
        slot = lax.rem(c, slots)
        acc[c] = jnp.zeros((pairs, width), jnp.float32)

        def step(k, carry):
            load(c, k).wait()
            at = pl.multiple_of(k * step_rows, step_rows)
            block = ibuf[slot, pl.ds(at, step_rows)].reshape(step_rows, width)
            acc[c] += jnp.dot(
                panel[:, pl.ds(at, step_rows)], block, preferred_element_type=jnp.float32
            )

            @pl.when(c + slots < chunks)
            def _():
                load(c + slots, k).start()

            return carry

        lax.fori_loop(0, blocks, step, 0)

        for side in (0, 1):
            @pl.when(place(side) == 0)
            def _():
                for t in range(1, n):
                    encode(part(c, owner_of(side, t)), sbuf.at[side, c, t - 1], width)
                    message(side, c, t).start()

    def forward(c, t):
        for side in (0, 1):
            @pl.when((place(side) > 0) & (place(side) < t))
            def _():
                message(side, c, t - 1).wait_recv()
                total = part(c, owner_of(side, t)) + decode(rbuf.at[side, c, t - 2], width)
                encode(total, sbuf.at[side, c, t - 1], width)
                message(side, c, t).start()

    def finish(c):
        for side in (0, 1):
            @pl.when(place(side) > 0)
            def _():
                message(side, c, n - 1).wait_recv()
                at = pl.ds(pl.multiple_of(z * rows, rows), rows)
                acc[c, at, :] += decode(rbuf.at[side, c, n - 2], width)
        held = pl.ds(pl.multiple_of(c * ca, ca), ca)
        base = base_ref[held, :].reshape(1, width)
        driver = driver_ref[:, held, :].astype(jnp.float32).reshape(rows, width)
        value = (part(c, z) + driver) / (pe_ref[:, :1] - base)
        value = jnp.where(base < OUTSIDE, value, 0.0)
        out_ref[:, held, :] = value.reshape(rows, ca, bwidth).astype(jnp.bfloat16)

    end_lag = n

    def turn(i, carry):
        @pl.when(i < chunks)
        def _():
            compute(i)

        for t in range(2, n):
            c = i - (t - 1)

            @pl.when((c >= 0) & (c < chunks))
            def _():
                forward(c, t)

        c = i - end_lag

        @pl.when(c >= 0)
        def _():
            finish(c)

        return carry

    lax.fori_loop(0, chunks + end_lag, turn, 0)
    lax.fori_loop(1, nv, done_share, 0)

    def done(c, carry):
        for side in (0, 1):
            for t in range(1, n):
                @pl.when((place(side) < t) & (place(side) < last))
                def _():
                    message(side, c, t).wait_send()
        return carry

    lax.fori_loop(0, chunks, done, 0)


def local(n, nv, amplitudes, integrals, driver, eps_occ, eps_vir, pair_occ, offsets, sizes):
    slab, a_count, bwidth = integrals.shape
    rows = driver.shape[0]
    pairs = rows * n
    ca = 16 if a_count % 16 == 0 else a_count
    chunks = a_count // ca
    width = ca * bwidth
    step_rows = 256 if slab % 256 == 0 else slab
    slots = min(4, chunks)

    vmem = pl.BlockSpec(memory_space=pltpu.VMEM)
    out = pl.pallas_call(
        functools.partial(kernel, n, nv, step_rows, slots),
        out_shape=jax.ShapeDtypeStruct(driver.shape, jnp.bfloat16),
        in_specs=[vmem, pl.BlockSpec(memory_space=pl.ANY)] + [vmem] * 7,
        out_specs=vmem,
        scratch_shapes=[
            pltpu.VMEM((nv, pairs // nv, slab), jnp.float32),
            pltpu.VMEM((pairs, slab), jnp.bfloat16),
            pltpu.VMEM((slots, slab, ca, bwidth), jnp.bfloat16),
            pltpu.VMEM((chunks, pairs, width), jnp.float32),
            pltpu.VMEM((2, chunks, n - 1, rows, width + LANES), jnp.int16),
            pltpu.VMEM((2, chunks, n - 1, rows, width + LANES), jnp.int16),
            pltpu.VMEM((rows, LANES), jnp.float32),
            pltpu.VMEM((a_count, bwidth), jnp.float32),
            pltpu.SemaphoreType.DMA((slots, slab // step_rows)),
            pltpu.SemaphoreType.DMA((nv,)),
            pltpu.SemaphoreType.DMA((nv,)),
            pltpu.SemaphoreType.DMA((2, chunks, n - 1)),
            pltpu.SemaphoreType.DMA((2, chunks, n - 1)),
        ],
        compiler_params=pltpu.CompilerParams(
            collective_id=0, has_side_effects=True, vmem_limit_bytes=56 * 1024 * 1024
        ),
        cost_estimate=pl.CostEstimate(
            flops=2 * pairs * slab * a_count * bwidth,
            bytes_accessed=2 * slab * a_count * bwidth,
            transcendentals=0,
        ),
    )(
        amplitudes, integrals, driver, eps_occ.reshape(1, -1), eps_vir.reshape(-1, bwidth),
        eps_vir.reshape(-1, a_count), pair_occ, offsets.reshape(1, -1), sizes.reshape(1, -1),
    )
    return out


def solution(mesh):
    placed = (
        P("virt", "opair"),
        P("opair", "virt", None),
        P("opair", "virt", None),
        P(),
        P(),
        P("opair", None),
        P("virt"),
        P("virt"),
    )
    return jax.shard_map(
        functools.partial(local, mesh.shape["opair"], mesh.shape["virt"]),
        mesh=mesh, in_specs=placed, out_specs=P("opair", "virt", None), check_vma=False,
    )
```

```python
import functools

import jax
import jax.numpy as jnp
from jax import lax
from jax.experimental import pallas as pl
from jax.experimental.pallas import tpu as pltpu
from jax.sharding import PartitionSpec as P

MESH = pl.DeviceIdType.MESH
LANES = 128
LEVELS = 32000.0
OUTSIDE = 1e30


def encode(x, out_ref, width):
    top = jnp.maximum(jnp.max(jnp.abs(x), axis=1, keepdims=True), 1e-30)
    code = jnp.broadcast_to(jnp.ceil(jnp.log2(top) * 64.0), (x.shape[0], LANES))
    gain = (jnp.exp2(code * (-1.0 / 64.0)) * LEVELS)[:, :1]
    out_ref[:, :width] = jnp.round(x * gain).astype(jnp.int32).astype(jnp.int16)
    out_ref[:, width:] = code.astype(jnp.int32).astype(jnp.int16)


def decode(in_ref, width):
    code = in_ref[:, width:].astype(jnp.int32).astype(jnp.float32)
    gain = (jnp.exp2(code * (1.0 / 64.0)) * (1.0 / LEVELS))[:, :1]
    return in_ref[:, :width].astype(jnp.int32).astype(jnp.float32) * gain


def kernel(
    n, nv, step_rows, slots,
    amp_ref, int_ref, driver_ref, occ_ref, vir_ref, own_ref, pair_ref, off_ref, size_ref, out_ref,
    panel32, panel, ibuf, acc, sbuf, rbuf, pe_ref, base_ref, order, turned,
    isem, asend, arecv, ssem, rsem,
):
    z = lax.axis_index("opair")
    v = lax.axis_index("virt")
    chunks, pairs, width = acc.shape
    rows = pairs // n
    slab, ca = ibuf.shape[1], ibuf.shape[2]
    last = n - 1

    bwidth = ibuf.shape[3]
    blocks = slab // step_rows

    def load(c, k):
        slot = lax.rem(c, slots)
        at = pl.ds(pl.multiple_of(k * step_rows, step_rows), step_rows)
        return pltpu.make_async_copy(
            int_ref.at[at, pl.ds(pl.multiple_of(c * ca, ca), ca), :], ibuf.at[slot, at], isem.at[slot, k]
        )

    for c in range(slots):
        for k in range(blocks):
            load(c, k).start()

    barrier = pltpu.get_barrier_semaphore()

    def greet(d, carry):
        peer = lax.rem(v + d, nv)
        pl.semaphore_signal(barrier, inc=1, device_id={"virt": peer}, device_id_type=MESH)
        return carry

    lax.fori_loop(1, nv, greet, 0)

    @pl.when(z > 0)
    def _():
        pl.semaphore_signal(barrier, inc=1, device_id={"opair": z - 1}, device_id_type=MESH)

    @pl.when(z < last)
    def _():
        pl.semaphore_signal(barrier, inc=1, device_id={"opair": z + 1}, device_id_type=MESH)

    depth = order.shape[0]
    group = depth // ca
    to = lax.broadcasted_iota(jnp.int32, (depth, depth), 0)
    source = lax.broadcasted_iota(jnp.int32, (depth, depth), 1)
    wanted = lax.rem(to, group) * ca + to // group
    order[...] = jnp.where(source == wanted, 1.0, 0.0).astype(jnp.bfloat16)
    panel32[v] = amp_ref[...].astype(jnp.float32)

    a_count = base_ref.shape[0]
    occupied = lax.broadcasted_iota(jnp.int32, (rows, occ_ref.shape[1]), 1)
    energy = jnp.zeros((rows, 1), jnp.float32)
    for j in (0, 1):
        hit = pair_ref[:, j:j + 1] == occupied
        energy += jnp.sum(jnp.where(hit, occ_ref[...], 0.0), axis=1, keepdims=True)
    pe_ref[...] = jnp.broadcast_to(energy, (rows, LANES))

    across = lax.broadcasted_iota(jnp.int32, (a_count, a_count), 1)
    same = lax.broadcasted_iota(jnp.int32, (a_count, a_count), 0) == across

    def column(x):
        return jnp.sum(jnp.where(same, x, 0.0), axis=1, keepdims=True)

    e_first = column(own_ref[pl.ds(v, 1), :])
    start = column(off_ref[...].astype(jnp.float32))
    size = column(size_ref[...].astype(jnp.float32))
    e_pair = jnp.zeros((a_count, bwidth), jnp.float32)
    for k in range(vir_ref.shape[0]):
        e_pair = jnp.where(start == float(k * bwidth), vir_ref[k:k + 1, :], e_pair)
    t_index = lax.broadcasted_iota(jnp.int32, (a_count, bwidth), 1).astype(jnp.float32)
    base_ref[...] = jnp.where(t_index < size, e_first + e_pair, OUTSIDE)
    beside = jnp.where(z > 0, 1, 0) + jnp.where(z < last, 1, 0)
    pl.semaphore_wait(barrier, nv - 1 + beside)

    def share(d, slot):
        peer = lax.rem(v + d, nv)
        return pltpu.make_async_remote_copy(
            src_ref=panel32.at[slot],
            dst_ref=panel32.at[slot],
            send_sem=asend.at[d],
            recv_sem=arecv.at[d],
            device_id={"virt": peer},
            device_id_type=MESH,
        )

    def start_share(d, carry):
        share(d, v).start()
        return carry

    def wait_share(d, carry):
        share(d, lax.rem(v - d + nv, nv)).wait_recv()
        return carry

    def done_share(d, carry):
        share(d, v).wait_send()
        return carry

    lax.fori_loop(1, nv, start_share, 0)
    lax.fori_loop(1, nv, wait_share, 0)
    panel[...] = panel32[...].reshape(pairs, slab).astype(jnp.bfloat16)

    def message(side, c, t):
        peer = lax.rem(z + 1, n) if side == 0 else lax.rem(z + last, n)
        return pltpu.make_async_remote_copy(
            src_ref=sbuf.at[side, c, t - 1],
            dst_ref=rbuf.at[side, c, t - 1],
            send_sem=ssem.at[side, c, t - 1],
            recv_sem=rsem.at[side, c, t - 1],
            device_id={"opair": peer},
            device_id_type=MESH,
        )

    def part(c, owner):
        return acc[c, pl.ds(pl.multiple_of(owner * rows, rows), rows), :]

    def place(side):
        return z if side == 0 else last - z

    def owner_of(side, t):
        o = place(side) + n - t
        return o if side == 0 else last - o

    def compute(c):
        slot = lax.rem(c, slots)
        acc[c] = jnp.zeros((pairs, width), jnp.float32)

        def step(k, carry):
            load(c, k).wait()
            at = pl.multiple_of(k * step_rows, step_rows)
            for b in range(0, step_rows, 2 * group):
                pair = [
                    ibuf[slot, pl.ds(at + b + j * group, group)].reshape(group * ca, bwidth)
                    for j in (0, 1)
                ]
                moved = jnp.dot(
                    order[...], jnp.concatenate(pair, axis=1), preferred_element_type=jnp.float32
                ).astype(jnp.bfloat16)
                for j in (0, 1):
                    turned[:, b + j * group:b + (j + 1) * group, :] = moved[
                        :, j * bwidth:(j + 1) * bwidth
                    ].reshape(ca, group, bwidth)
            block = jnp.concatenate([turned[a] for a in range(ca)], axis=1)
            acc[c] += jnp.dot(
                panel[:, pl.ds(at, step_rows)], block, preferred_element_type=jnp.float32
            )

            @pl.when(c + slots < chunks)
            def _():
                load(c + slots, k).start()

            return carry

        lax.fori_loop(0, blocks, step, 0)

        for side in (0, 1):
            @pl.when(place(side) == 0)
            def _():
                for t in range(1, n):
                    encode(part(c, owner_of(side, t)), sbuf.at[side, c, t - 1], width)
                    message(side, c, t).start()

    def forward(c, t):
        for side in (0, 1):
            @pl.when((place(side) > 0) & (place(side) < t))
            def _():
                message(side, c, t - 1).wait_recv()
                total = part(c, owner_of(side, t)) + decode(rbuf.at[side, c, t - 2], width)
                encode(total, sbuf.at[side, c, t - 1], width)
                message(side, c, t).start()

    def finish(c):
        for side in (0, 1):
            @pl.when(place(side) > 0)
            def _():
                message(side, c, n - 1).wait_recv()
                at = pl.ds(pl.multiple_of(z * rows, rows), rows)
                acc[c, at, :] += decode(rbuf.at[side, c, n - 2], width)
        held = pl.ds(pl.multiple_of(c * ca, ca), ca)
        base = base_ref[held, :].reshape(1, width)
        driver = driver_ref[:, held, :].astype(jnp.float32).reshape(rows, width)
        value = (part(c, z) + driver) / (pe_ref[:, :1] - base)
        value = jnp.where(base < OUTSIDE, value, 0.0)
        out_ref[:, held, :] = value.reshape(rows, ca, bwidth).astype(jnp.bfloat16)

    end_lag = n

    def turn(i, carry):
        @pl.when(i < chunks)
        def _():
            compute(i)

        for t in range(2, n):
            c = i - (t - 1)

            @pl.when((c >= 0) & (c < chunks))
            def _():
                forward(c, t)

        c = i - end_lag

        @pl.when(c >= 0)
        def _():
            finish(c)

        return carry

    lax.fori_loop(0, chunks + end_lag, turn, 0)
    lax.fori_loop(1, nv, done_share, 0)

    def done(c, carry):
        for side in (0, 1):
            for t in range(1, n):
                @pl.when((place(side) < t) & (place(side) < last))
                def _():
                    message(side, c, t).wait_send()
        return carry

    lax.fori_loop(0, chunks, done, 0)


def local(n, nv, amplitudes, integrals, driver, eps_occ, eps_vir, pair_occ, offsets, sizes):
    slab, a_count, bwidth = integrals.shape
    rows = driver.shape[0]
    pairs = rows * n
    ca = 16 if a_count % 16 == 0 else a_count
    chunks = a_count // ca
    width = ca * bwidth
    step_rows = 512 if slab % 512 == 0 else slab
    depth = 256
    slots = min(4, chunks)

    vmem = pl.BlockSpec(memory_space=pltpu.VMEM)
    out = pl.pallas_call(
        functools.partial(kernel, n, nv, step_rows, slots),
        out_shape=jax.ShapeDtypeStruct(driver.shape, jnp.bfloat16),
        in_specs=[vmem, pl.BlockSpec(memory_space=pl.ANY)] + [vmem] * 7,
        out_specs=vmem,
        scratch_shapes=[
            pltpu.VMEM((nv, pairs // nv, slab), jnp.float32),
            pltpu.VMEM((pairs, slab), jnp.bfloat16),
            pltpu.VMEM((slots, slab, ca, bwidth), jnp.bfloat16),
            pltpu.VMEM((chunks, pairs, width), jnp.float32),
            pltpu.VMEM((2, chunks, n - 1, rows, width + LANES), jnp.int16),
            pltpu.VMEM((2, chunks, n - 1, rows, width + LANES), jnp.int16),
            pltpu.VMEM((rows, LANES), jnp.float32),
            pltpu.VMEM((a_count, bwidth), jnp.float32),
            pltpu.VMEM((depth, depth), jnp.bfloat16),
            pltpu.VMEM((ca, step_rows, bwidth), jnp.bfloat16),
            pltpu.SemaphoreType.DMA((slots, slab // step_rows)),
            pltpu.SemaphoreType.DMA((nv,)),
            pltpu.SemaphoreType.DMA((nv,)),
            pltpu.SemaphoreType.DMA((2, chunks, n - 1)),
            pltpu.SemaphoreType.DMA((2, chunks, n - 1)),
        ],
        compiler_params=pltpu.CompilerParams(
            collective_id=0, has_side_effects=True, vmem_limit_bytes=56 * 1024 * 1024
        ),
        cost_estimate=pl.CostEstimate(
            flops=2 * pairs * slab * a_count * bwidth,
            bytes_accessed=2 * slab * a_count * bwidth,
            transcendentals=0,
        ),
    )(
        amplitudes, integrals, driver, eps_occ.reshape(1, -1), eps_vir.reshape(-1, bwidth),
        eps_vir.reshape(-1, a_count), pair_occ, offsets.reshape(1, -1), sizes.reshape(1, -1),
    )
    return out


def solution(mesh):
    placed = (
        P("virt", "opair"),
        P("opair", "virt", None),
        P("opair", "virt", None),
        P(),
        P(),
        P("opair", None),
        P("virt"),
        P("virt"),
    )
    return jax.shard_map(
        functools.partial(local, mesh.shape["opair"], mesh.shape["virt"]),
        mesh=mesh, in_specs=placed, out_specs=P("opair", "virt", None), check_vma=False,
    )
```

```python
import functools

import jax
import jax.numpy as jnp
from jax import lax
from jax.experimental import pallas as pl
from jax.experimental.pallas import tpu as pltpu
from jax.sharding import PartitionSpec as P

MESH = pl.DeviceIdType.MESH
LANES = 128
LEVELS = 32000.0
OUTSIDE = 1e30


def encode(x, out_ref, width):
    top = jnp.maximum(jnp.max(jnp.abs(x), axis=1, keepdims=True), 1e-30)
    code = jnp.broadcast_to(jnp.ceil(jnp.log2(top) * 64.0), (x.shape[0], LANES))
    gain = (jnp.exp2(code * (-1.0 / 64.0)) * LEVELS)[:, :1]
    out_ref[:, :width] = jnp.round(x * gain).astype(jnp.int32).astype(jnp.int16)
    out_ref[:, width:] = code.astype(jnp.int32).astype(jnp.int16)


def decode(in_ref, width):
    code = in_ref[:, width:].astype(jnp.int32).astype(jnp.float32)
    gain = (jnp.exp2(code * (1.0 / 64.0)) * (1.0 / LEVELS))[:, :1]
    return in_ref[:, :width].astype(jnp.int32).astype(jnp.float32) * gain


def kernel(
    n, nv, step_rows, slots,
    amp_ref, int_ref, driver_ref, occ_ref, vir_ref, own_ref, pair_ref, off_ref, size_ref, out_ref,
    panel32, panel, ibuf, acc, sbuf, rbuf, pe_ref, base_ref, order, turned,
    isem, asend, arecv, ssem, rsem,
):
    z = lax.axis_index("opair")
    v = lax.axis_index("virt")
    chunks, pairs, width = acc.shape
    rows = pairs // n
    slab, ca = ibuf.shape[1], ibuf.shape[2]
    last = n - 1

    bwidth = ibuf.shape[3]
    blocks = slab // step_rows

    def load(c, k):
        slot = lax.rem(c, slots)
        at = pl.ds(pl.multiple_of(k * step_rows, step_rows), step_rows)
        return pltpu.make_async_copy(
            int_ref.at[at, pl.ds(pl.multiple_of(c * ca, ca), ca), :], ibuf.at[slot, at], isem.at[slot, k]
        )

    for c in range(slots):
        for k in range(blocks):
            load(c, k).start()

    barrier = pltpu.get_barrier_semaphore()

    def greet(d, carry):
        peer = lax.rem(v + d, nv)
        pl.semaphore_signal(barrier, inc=1, device_id={"virt": peer}, device_id_type=MESH)
        return carry

    lax.fori_loop(1, nv, greet, 0)

    @pl.when(z > 0)
    def _():
        pl.semaphore_signal(barrier, inc=1, device_id={"opair": z - 1}, device_id_type=MESH)

    @pl.when(z < last)
    def _():
        pl.semaphore_signal(barrier, inc=1, device_id={"opair": z + 1}, device_id_type=MESH)

    panel32[v] = amp_ref[...].astype(jnp.float32)
    beside = jnp.where(z > 0, 1, 0) + jnp.where(z < last, 1, 0)
    pl.semaphore_wait(barrier, nv - 1 + beside)

    def share(d, slot):
        peer = lax.rem(v + d, nv)
        return pltpu.make_async_remote_copy(
            src_ref=panel32.at[slot],
            dst_ref=panel32.at[slot],
            send_sem=asend.at[d],
            recv_sem=arecv.at[d],
            device_id={"virt": peer},
            device_id_type=MESH,
        )

    def start_share(d, carry):
        share(d, v).start()
        return carry

    def wait_share(d, carry):
        share(d, lax.rem(v - d + nv, nv)).wait_recv()
        return carry

    def done_share(d, carry):
        share(d, v).wait_send()
        return carry

    lax.fori_loop(1, nv, start_share, 0)

    depth = order.shape[0]
    group = depth // ca
    to = lax.broadcasted_iota(jnp.int32, (depth, depth), 0)
    source = lax.broadcasted_iota(jnp.int32, (depth, depth), 1)
    wanted = lax.rem(to, group) * ca + to // group
    order[...] = jnp.where(source == wanted, 1.0, 0.0).astype(jnp.bfloat16)

    a_count = base_ref.shape[0]
    def column(x):
        size = x.shape[1]
        across = lax.broadcasted_iota(jnp.int32, (size, size), 1)
        same = lax.broadcasted_iota(jnp.int32, (size, size), 0) == across
        return jnp.sum(jnp.where(same, x.astype(jnp.float32), 0.0), axis=1, keepdims=True)

    occupied = lax.broadcasted_iota(jnp.int32, (rows, occ_ref.shape[1]), 1).astype(jnp.float32)
    energy = jnp.zeros((rows, 1), jnp.float32)
    for j in (0, 1):
        hit = column(pair_ref[j:j + 1, :]) == occupied
        energy += jnp.sum(jnp.where(hit, occ_ref[...], 0.0), axis=1, keepdims=True)
    pe_ref[...] = jnp.broadcast_to(energy, (rows, LANES))

    e_first = column(own_ref[pl.ds(v, 1), :])
    start = column(off_ref[...])
    size = column(size_ref[...])
    e_pair = jnp.zeros((a_count, bwidth), jnp.float32)
    for k in range(vir_ref.shape[0]):
        e_pair = jnp.where(start == float(k * bwidth), vir_ref[k:k + 1, :], e_pair)
    t_index = lax.broadcasted_iota(jnp.int32, (a_count, bwidth), 1).astype(jnp.float32)
    base_ref[...] = jnp.where(t_index < size, e_first + e_pair, OUTSIDE)

    def reorder(c, k):
        load(c, k).wait()
        slot = lax.rem(c, slots)
        at = pl.multiple_of(k * step_rows, step_rows)
        for b in range(0, step_rows, 2 * group):
            pair = [
                ibuf[slot, pl.ds(at + b + j * group, group)].reshape(group * ca, bwidth)
                for j in (0, 1)
            ]
            moved = jnp.dot(
                order[...], jnp.concatenate(pair, axis=1), preferred_element_type=jnp.float32
            ).astype(jnp.bfloat16)
            for j in (0, 1):
                turned[k, :, b + j * group:b + (j + 1) * group, :] = moved[
                    :, j * bwidth:(j + 1) * bwidth
                ].reshape(ca, group, bwidth)

        @pl.when(c + slots < chunks)
        def _():
            load(c + slots, k).start()

    def reorder_first(k, carry):
        reorder(0, k)
        return carry

    lax.fori_loop(0, blocks, reorder_first, 0)
    lax.fori_loop(1, nv, wait_share, 0)
    panel[...] = panel32[...].reshape(pairs, slab).astype(jnp.bfloat16)

    def message(side, c, t):
        peer = lax.rem(z + 1, n) if side == 0 else lax.rem(z + last, n)
        return pltpu.make_async_remote_copy(
            src_ref=sbuf.at[side, c, t - 1],
            dst_ref=rbuf.at[side, c, t - 1],
            send_sem=ssem.at[side, c, t - 1],
            recv_sem=rsem.at[side, c, t - 1],
            device_id={"opair": peer},
            device_id_type=MESH,
        )

    def part(c, owner):
        return acc[c, pl.ds(pl.multiple_of(owner * rows, rows), rows), :]

    def place(side):
        return z if side == 0 else last - z

    def owner_of(side, t):
        o = place(side) + n - t
        return o if side == 0 else last - o

    def compute(c):
        acc[c] = jnp.zeros((pairs, width), jnp.float32)

        def step(k, carry):
            @pl.when(c > 0)
            def _():
                reorder(c, k)

            at = pl.multiple_of(k * step_rows, step_rows)
            block = jnp.concatenate([turned[k, a] for a in range(ca)], axis=1)
            acc[c] += jnp.dot(
                panel[:, pl.ds(at, step_rows)], block, preferred_element_type=jnp.float32
            )
            return carry

        lax.fori_loop(0, blocks, step, 0)

        for side in (0, 1):
            @pl.when(place(side) == 0)
            def _():
                for t in range(1, n):
                    encode(part(c, owner_of(side, t)), sbuf.at[side, c, t - 1], width)
                    message(side, c, t).start()

    def forward(c, t):
        for side in (0, 1):
            @pl.when((place(side) > 0) & (place(side) < t))
            def _():
                message(side, c, t - 1).wait_recv()
                total = part(c, owner_of(side, t)) + decode(rbuf.at[side, c, t - 2], width)
                encode(total, sbuf.at[side, c, t - 1], width)
                message(side, c, t).start()

    def finish(c):
        for side in (0, 1):
            @pl.when(place(side) > 0)
            def _():
                message(side, c, n - 1).wait_recv()
                at = pl.ds(pl.multiple_of(z * rows, rows), rows)
                acc[c, at, :] += decode(rbuf.at[side, c, n - 2], width)
        held = pl.ds(pl.multiple_of(c * ca, ca), ca)
        base = base_ref[held, :].reshape(1, width)
        driver = driver_ref[:, held, :].astype(jnp.float32).reshape(rows, width)
        value = (part(c, z) + driver) / (pe_ref[:, :1] - base)
        value = jnp.where(base < OUTSIDE, value, 0.0)
        out_ref[:, held, :] = value.reshape(rows, ca, bwidth)

    end_lag = n

    def turn(i, carry):
        @pl.when(i < chunks)
        def _():
            compute(i)

        for t in range(2, n):
            c = i - (t - 1)

            @pl.when((c >= 0) & (c < chunks))
            def _():
                forward(c, t)

        c = i - end_lag

        @pl.when(c >= 0)
        def _():
            finish(c)

        return carry

    lax.fori_loop(0, chunks + end_lag, turn, 0)
    lax.fori_loop(1, nv, done_share, 0)

    def done(c, carry):
        for side in (0, 1):
            for t in range(1, n):
                @pl.when((place(side) < t) & (place(side) < last))
                def _():
                    message(side, c, t).wait_send()
        return carry

    lax.fori_loop(0, chunks, done, 0)


def local(n, nv, amplitudes, integrals, driver, eps_occ, eps_vir, pair_occ, offsets, sizes):
    slab, a_count, bwidth = integrals.shape
    rows = driver.shape[0]
    pairs = rows * n
    ca = 16 if a_count % 16 == 0 else a_count
    chunks = a_count // ca
    width = ca * bwidth
    step_rows = 512 if slab % 512 == 0 else slab
    depth = 256
    slots = min(4, chunks)

    vmem = pl.BlockSpec(memory_space=pltpu.VMEM)
    out = pl.pallas_call(
        functools.partial(kernel, n, nv, step_rows, slots),
        out_shape=jax.ShapeDtypeStruct(driver.shape, jnp.float32),
        in_specs=[vmem, pl.BlockSpec(memory_space=pl.ANY)] + [vmem] * 7,
        out_specs=vmem,
        scratch_shapes=[
            pltpu.VMEM((nv, pairs // nv, slab), jnp.float32),
            pltpu.VMEM((pairs, slab), jnp.bfloat16),
            pltpu.VMEM((slots, slab, ca, bwidth), jnp.bfloat16),
            pltpu.VMEM((chunks, pairs, width), jnp.float32),
            pltpu.VMEM((2, chunks, n - 1, rows, width + LANES), jnp.int16),
            pltpu.VMEM((2, chunks, n - 1, rows, width + LANES), jnp.int16),
            pltpu.VMEM((rows, LANES), jnp.float32),
            pltpu.VMEM((a_count, bwidth), jnp.float32),
            pltpu.VMEM((depth, depth), jnp.bfloat16),
            pltpu.VMEM((slab // step_rows, ca, step_rows, bwidth), jnp.bfloat16),
            pltpu.SemaphoreType.DMA((slots, slab // step_rows)),
            pltpu.SemaphoreType.DMA((nv,)),
            pltpu.SemaphoreType.DMA((nv,)),
            pltpu.SemaphoreType.DMA((2, chunks, n - 1)),
            pltpu.SemaphoreType.DMA((2, chunks, n - 1)),
        ],
        compiler_params=pltpu.CompilerParams(
            collective_id=0, has_side_effects=True, vmem_limit_bytes=56 * 1024 * 1024
        ),
        cost_estimate=pl.CostEstimate(
            flops=2 * pairs * slab * a_count * bwidth,
            bytes_accessed=2 * slab * a_count * bwidth,
            transcendentals=0,
        ),
    )(
        amplitudes, integrals, driver, eps_occ.reshape(1, -1), eps_vir.reshape(-1, bwidth),
        eps_vir.reshape(-1, a_count), pair_occ.T, offsets.reshape(1, -1), sizes.reshape(1, -1),
    )
    return out.astype(jnp.bfloat16)


def solution(mesh):
    placed = (
        P("virt", "opair"),
        P("opair", "virt", None),
        P("opair", "virt", None),
        P(),
        P(),
        P("opair", None),
        P("virt"),
        P("virt"),
    )
    return jax.shard_map(
        functools.partial(local, mesh.shape["opair"], mesh.shape["virt"]),
        mesh=mesh, in_specs=placed, out_specs=P("opair", "virt", None), check_vma=False,
    )
```

```python
import functools

import jax
import jax.numpy as jnp
from jax import lax
from jax.experimental import pallas as pl
from jax.experimental.pallas import tpu as pltpu
from jax.sharding import PartitionSpec as P

MESH = pl.DeviceIdType.MESH
LANES = 128
LEVELS = 32000.0
OUTSIDE = 1e30


def diagonal(rows, lanes):
    return lax.broadcasted_iota(jnp.int32, (rows, lanes), 0) == lax.broadcasted_iota(
        jnp.int32, (rows, lanes), 1
    )


def encode(x, out_ref, top_ref):
    top = jnp.maximum(jnp.max(jnp.abs(x), axis=1, keepdims=True), 1e-30)
    same = diagonal(x.shape[0], top_ref.shape[1])
    top_ref[...] = jnp.sum(jnp.where(same, top, 0.0), axis=0, keepdims=True)
    out_ref[...] = jnp.round(x * (LEVELS / top)).astype(jnp.int32).astype(jnp.int16)


def decode(in_ref, top_ref):
    same = diagonal(in_ref.shape[0], top_ref.shape[1])
    top = jnp.sum(jnp.where(same, top_ref[...], 0.0), axis=1, keepdims=True)
    return in_ref[...].astype(jnp.int32).astype(jnp.float32) * (top * (1.0 / LEVELS))


def kernel(
    n, nv, step_rows, slots,
    amp_ref, int_ref, driver_ref, occ_ref, vir_ref, own_ref, pair_ref, off_ref, size_ref, out_ref,
    panel32, panel, ibuf, acc, sbuf, rbuf, stop, rtop, pe_ref, base_ref, order, turned,
    isem, asend, arecv, ssem, rsem, stsem, rtsem,
):
    z = lax.axis_index("opair")
    v = lax.axis_index("virt")
    chunks, pairs, width = acc.shape
    rows = pairs // n
    slab, ca = ibuf.shape[1], ibuf.shape[2]
    last = n - 1

    bwidth = ibuf.shape[3]
    blocks = slab // step_rows

    def load(c, k):
        slot = lax.rem(c, slots)
        at = pl.ds(pl.multiple_of(k * step_rows, step_rows), step_rows)
        return pltpu.make_async_copy(
            int_ref.at[at, pl.ds(pl.multiple_of(c * ca, ca), ca), :], ibuf.at[slot, at], isem.at[slot, k]
        )

    for c in range(slots):
        for k in range(blocks):
            load(c, k).start()

    barrier = pltpu.get_barrier_semaphore()

    def greet(d, carry):
        peer = lax.rem(v + d, nv)
        pl.semaphore_signal(barrier, inc=1, device_id={"virt": peer}, device_id_type=MESH)
        return carry

    lax.fori_loop(1, nv, greet, 0)

    @pl.when(z > 0)
    def _():
        pl.semaphore_signal(barrier, inc=1, device_id={"opair": z - 1}, device_id_type=MESH)

    @pl.when(z < last)
    def _():
        pl.semaphore_signal(barrier, inc=1, device_id={"opair": z + 1}, device_id_type=MESH)

    panel32[v] = amp_ref[...].astype(jnp.float32)
    beside = jnp.where(z > 0, 1, 0) + jnp.where(z < last, 1, 0)
    pl.semaphore_wait(barrier, nv - 1 + beside)

    def share(d, slot):
        peer = lax.rem(v + d, nv)
        return pltpu.make_async_remote_copy(
            src_ref=panel32.at[slot],
            dst_ref=panel32.at[slot],
            send_sem=asend.at[d],
            recv_sem=arecv.at[d],
            device_id={"virt": peer},
            device_id_type=MESH,
        )

    def start_share(d, carry):
        share(d, v).start()
        return carry

    def wait_share(d, carry):
        share(d, lax.rem(v - d + nv, nv)).wait_recv()
        return carry

    def done_share(d, carry):
        share(d, v).wait_send()
        return carry

    lax.fori_loop(1, nv, start_share, 0)

    depth = order.shape[0]
    group = depth // ca
    to = lax.broadcasted_iota(jnp.int32, (depth, depth), 0)
    source = lax.broadcasted_iota(jnp.int32, (depth, depth), 1)
    wanted = lax.rem(to, group) * ca + to // group
    order[...] = jnp.where(source == wanted, 1.0, 0.0).astype(jnp.bfloat16)

    a_count = base_ref.shape[0]
    def column(x):
        size = x.shape[1]
        across = lax.broadcasted_iota(jnp.int32, (size, size), 1)
        same = lax.broadcasted_iota(jnp.int32, (size, size), 0) == across
        return jnp.sum(jnp.where(same, x.astype(jnp.float32), 0.0), axis=1, keepdims=True)

    occupied = lax.broadcasted_iota(jnp.int32, (rows, occ_ref.shape[1]), 1).astype(jnp.float32)
    energy = jnp.zeros((rows, 1), jnp.float32)
    for j in (0, 1):
        hit = column(pair_ref[j:j + 1, :]) == occupied
        energy += jnp.sum(jnp.where(hit, occ_ref[...], 0.0), axis=1, keepdims=True)
    pe_ref[...] = jnp.broadcast_to(energy, (rows, LANES))

    e_first = column(own_ref[pl.ds(v, 1), :])
    start = column(off_ref[...])
    size = column(size_ref[...])
    e_pair = jnp.zeros((a_count, bwidth), jnp.float32)
    for k in range(vir_ref.shape[0]):
        e_pair = jnp.where(start == float(k * bwidth), vir_ref[k:k + 1, :], e_pair)
    t_index = lax.broadcasted_iota(jnp.int32, (a_count, bwidth), 1).astype(jnp.float32)
    base_ref[...] = jnp.where(t_index < size, e_first + e_pair, OUTSIDE)

    def reorder(c, k):
        load(c, k).wait()
        slot = lax.rem(c, slots)
        at = pl.multiple_of(k * step_rows, step_rows)
        for b in range(0, step_rows, 2 * group):
            pair = [
                ibuf[slot, pl.ds(at + b + j * group, group)].reshape(group * ca, bwidth)
                for j in (0, 1)
            ]
            moved = jnp.dot(
                order[...], jnp.concatenate(pair, axis=1), preferred_element_type=jnp.float32
            ).astype(jnp.bfloat16)
            for j in (0, 1):
                turned[k, :, b + j * group:b + (j + 1) * group, :] = moved[
                    :, j * bwidth:(j + 1) * bwidth
                ].reshape(ca, group, bwidth)

        @pl.when(c + slots < chunks)
        def _():
            load(c + slots, k).start()

    def reorder_first(k, carry):
        reorder(0, k)
        return carry

    lax.fori_loop(0, blocks, reorder_first, 0)
    lax.fori_loop(1, nv, wait_share, 0)
    panel[...] = panel32[...].reshape(pairs, slab).astype(jnp.bfloat16)

    def messages(side, c, t):
        peer = lax.rem(z + 1, n) if side == 0 else lax.rem(z + last, n)
        return [
            pltpu.make_async_remote_copy(
                src_ref=source.at[side, c, t - 1],
                dst_ref=target.at[side, c, t - 1],
                send_sem=send.at[side, c, t - 1],
                recv_sem=receive.at[side, c, t - 1],
                device_id={"opair": peer},
                device_id_type=MESH,
            )
            for source, target, send, receive in (
                (stop, rtop, stsem, rtsem), (sbuf, rbuf, ssem, rsem),
            )
        ]

    def send(side, c, t, total):
        encode(total, sbuf.at[side, c, t - 1], stop.at[side, c, t - 1])
        for copy in messages(side, c, t):
            copy.start()

    def receive(side, c, t):
        for copy in messages(side, c, t):
            copy.wait_recv()
        return decode(rbuf.at[side, c, t - 1], rtop.at[side, c, t - 1])

    def part(c, owner):
        return acc[c, pl.ds(pl.multiple_of(owner * rows, rows), rows), :]

    def place(side):
        return z if side == 0 else last - z

    def owner_of(side, t):
        o = place(side) + n - t
        return o if side == 0 else last - o

    def compute(c):
        acc[c] = jnp.zeros((pairs, width), jnp.float32)

        def step(k, carry):
            @pl.when(c > 0)
            def _():
                reorder(c, k)

            at = pl.multiple_of(k * step_rows, step_rows)
            block = jnp.concatenate([turned[k, a] for a in range(ca)], axis=1)
            acc[c] += jnp.dot(
                panel[:, pl.ds(at, step_rows)], block, preferred_element_type=jnp.float32
            )
            return carry

        lax.fori_loop(0, blocks, step, 0)

        for side in (0, 1):
            @pl.when(place(side) == 0)
            def _():
                for t in range(1, n):
                    send(side, c, t, part(c, owner_of(side, t)))

    def forward(c, t):
        for side in (0, 1):
            @pl.when((place(side) > 0) & (place(side) < t))
            def _():
                send(side, c, t, part(c, owner_of(side, t)) + receive(side, c, t - 1))

    def finish(c):
        for side in (0, 1):
            @pl.when(place(side) > 0)
            def _():
                arrived = receive(side, c, n - 1)
                at = pl.ds(pl.multiple_of(z * rows, rows), rows)
                acc[c, at, :] += arrived
        held = pl.ds(pl.multiple_of(c * ca, ca), ca)
        base = base_ref[held, :].reshape(1, width)
        driver = driver_ref[:, held, :].astype(jnp.float32).reshape(rows, width)
        value = (part(c, z) + driver) / (pe_ref[:, :1] - base)
        value = jnp.where(base < OUTSIDE, value, 0.0)
        out_ref[:, held, :] = value.reshape(rows, ca, bwidth).astype(jnp.bfloat16)

    end_lag = n

    def turn(i, carry):
        @pl.when(i < chunks)
        def _():
            compute(i)

        for t in range(2, n):
            c = i - (t - 1)

            @pl.when((c >= 0) & (c < chunks))
            def _():
                forward(c, t)

        c = i - end_lag

        @pl.when(c >= 0)
        def _():
            finish(c)

        return carry

    lax.fori_loop(0, chunks + end_lag, turn, 0)
    lax.fori_loop(1, nv, done_share, 0)

    def done(c, carry):
        for side in (0, 1):
            for t in range(1, n):
                @pl.when((place(side) < t) & (place(side) < last))
                def _():
                    for copy in messages(side, c, t):
                        copy.wait_send()
        return carry

    lax.fori_loop(0, chunks, done, 0)


def local(n, nv, amplitudes, integrals, driver, eps_occ, eps_vir, pair_occ, offsets, sizes):
    slab, a_count, bwidth = integrals.shape
    rows = driver.shape[0]
    pairs = rows * n
    ca = 16 if a_count % 16 == 0 else a_count
    chunks = a_count // ca
    width = ca * bwidth
    step_rows = 512 if slab % 512 == 0 else slab
    depth = 256
    slots = min(4, chunks)
    tops = -(-rows // LANES) * LANES

    vmem = pl.BlockSpec(memory_space=pltpu.VMEM)
    out = pl.pallas_call(
        functools.partial(kernel, n, nv, step_rows, slots),
        out_shape=jax.ShapeDtypeStruct(driver.shape, jnp.bfloat16),
        in_specs=[vmem, pl.BlockSpec(memory_space=pl.ANY)] + [vmem] * 7,
        out_specs=vmem,
        scratch_shapes=[
            pltpu.VMEM((nv, pairs // nv, slab), jnp.float32),
            pltpu.VMEM((pairs, slab), jnp.bfloat16),
            pltpu.VMEM((slots, slab, ca, bwidth), jnp.bfloat16),
            pltpu.VMEM((chunks, pairs, width), jnp.float32),
            pltpu.VMEM((2, chunks, n - 1, rows, width), jnp.int16),
            pltpu.VMEM((2, chunks, n - 1, rows, width), jnp.int16),
            pltpu.VMEM((2, chunks, n - 1, 1, tops), jnp.float32),
            pltpu.VMEM((2, chunks, n - 1, 1, tops), jnp.float32),
            pltpu.VMEM((rows, LANES), jnp.float32),
            pltpu.VMEM((a_count, bwidth), jnp.float32),
            pltpu.VMEM((depth, depth), jnp.bfloat16),
            pltpu.VMEM((slab // step_rows, ca, step_rows, bwidth), jnp.bfloat16),
            pltpu.SemaphoreType.DMA((slots, slab // step_rows)),
            pltpu.SemaphoreType.DMA((nv,)),
            pltpu.SemaphoreType.DMA((nv,)),
            pltpu.SemaphoreType.DMA((2, chunks, n - 1)),
            pltpu.SemaphoreType.DMA((2, chunks, n - 1)),
            pltpu.SemaphoreType.DMA((2, chunks, n - 1)),
            pltpu.SemaphoreType.DMA((2, chunks, n - 1)),
        ],
        compiler_params=pltpu.CompilerParams(
            collective_id=0, has_side_effects=True, vmem_limit_bytes=56 * 1024 * 1024
        ),
        cost_estimate=pl.CostEstimate(
            flops=2 * pairs * slab * a_count * bwidth,
            bytes_accessed=2 * slab * a_count * bwidth,
            transcendentals=0,
        ),
    )(
        amplitudes, integrals, driver, eps_occ.reshape(1, -1), eps_vir.reshape(-1, bwidth),
        eps_vir.reshape(-1, a_count), pair_occ.T, offsets.reshape(1, -1), sizes.reshape(1, -1),
    )
    return out


def solution(mesh):
    placed = (
        P("virt", "opair"),
        P("opair", "virt", None),
        P("opair", "virt", None),
        P(),
        P(),
        P("opair", None),
        P("virt"),
        P("virt"),
    )
    return jax.shard_map(
        functools.partial(local, mesh.shape["opair"], mesh.shape["virt"]),
        mesh=mesh, in_specs=placed, out_specs=P("opair", "virt", None), check_vma=False,
    )
```
